32 devices in a mesh: seq: 8 (over z, x), tp: 4 (over y, core).
Axes of the slice: x: 2, y: 2, z: 4, core: 2. Of those that a mesh axis runs over, the one named last changes fastest.
Arguments:
- hidden: bfloat16 [4096, 4608], P('seq', 'tp'), may hold values from -60 to 60, as said below
- norm_gain: float32 [4608], replicated, may hold values from 0.1 to 1.9
- w_query: bfloat16 [4608, 2048], P(None, 'tp'), may hold values from -0.25 to 0.25
- w_key: bfloat16 [4608, 1024], P(None, 'tp'), may hold values from -0.09375 to 0.09375
- w_value: bfloat16 [4608, 1024], P(None, 'tp'), may hold values from -0.09375 to 0.09375
- segment_ids: int32 [4096], P('seq'), may hold values from 0 to 1, as said below
- page_table: int32 [8, 4], P('seq'), may hold values from 0 to 3, each once within a row
Outputs:
- attended: bfloat16 [4096, 2048], P('seq', 'tp')
- kv_cache: bfloat16 [32, 128, 2, 1024], P(('seq', 'tp'))
The draws below stay inside these ranges and needn't reach their ends.
Inputs may be any that keep to these rules, and one draw needn't show every extreme that they name: hidden is finite. `segment_ids`: never falling along the stream and rising by one at each document start; every number from 0 to 1 appears; no document is longer than 4096 tokens. `page_table`: each row holds every number from 0 to 3 once.
All inputs are finite; a program needn't handle non-finite values.
Results may differ from the reference program's by a relative error of at most 0.012.
The reference program's roundings to bfloat16 on the way count: a program that leaves them out, or rounds other values in their place, can miss the bound.
Values may be sent and summed in bfloat16 or wider, within the bound.
A program may use at most 128 MiB of HBM per device.

```python
import jax
import jax.numpy as jnp
from jax import lax

D = 4608
QH = 16
KVH = 8
HD = 128
WIN = 4096
PAGE = 128
TOK_DEV = 512
STREAM = 4096
PAGES_DEV = 4
NPAGES = 32
SEGS = 2
N_SEQ = 8


def draw_hidden(key, part):
    key_base, key_cols, key_rows = jax.random.split(key, 3)
    columns = jnp.arange(D, dtype=jnp.float32)
    rising = jnp.exp(jnp.log(3.0) * columns / D) * jax.random.uniform(key_cols, (D,), jnp.float32, 0.7, 1.4)
    row_scales = jnp.exp(jax.random.uniform(key_rows, (STREAM, 1), jnp.float32, 0.0, jnp.log(10.0)))
    base = jnp.clip(jax.random.normal(key_base, (STREAM, D), jnp.float32), -4.0, 4.0)
    return (base * row_scales * rising[None, :] * 0.25).astype(jnp.bfloat16)


def draw_segment_ids(key, part):
    key_offsets, key_middle = jax.random.split(jax.random.fold_in(key, 7), 2)
    half_win = WIN // 2
    base_points = jnp.arange(1, SEGS, dtype=jnp.int32) * half_win
    offsets = jax.random.randint(key_offsets, (SEGS - 1,), 1, half_win, dtype=jnp.int32)
    middle_offset = jax.random.randint(key_middle, (), 1, min(TOK_DEV, half_win), dtype=jnp.int32)
    offsets = offsets.at[SEGS // 2 - 1].set(middle_offset)
    bounds = base_points + offsets
    bounds = jnp.where(bounds % TOK_DEV == 0, bounds + 1, bounds)
    token_index = jnp.arange(STREAM, dtype=jnp.int32)
    return jnp.sum((token_index[:, None] >= bounds[None, :]).astype(jnp.int32), axis=1).astype(jnp.int32)


def level_of(key, shape, cuts, low, high):
    gain = 1.0
    for axis_at, blocks in cuts:
        draws = jax.random.uniform(jax.random.fold_in(jax.random.fold_in(key, 6), axis_at), (blocks,), jnp.float32, low / len(cuts), high / len(cuts))
        gain = gain * jnp.repeat(jnp.exp(draws), shape[axis_at] // blocks).reshape((-1,) + (1,) * (len(shape) - 1 - axis_at))
    return gain


def gaussian(key, dims, deviation, reach, pieces=(), kind=jnp.bfloat16):
    array = jax.random.normal(key, dims, jnp.float32) * deviation
    if len(pieces) > 0:
        array = level_of(key, dims, pieces, -0.22, 0.18) * array
    return jnp.clip(array, min=-reach, max=reach).astype(kind)


def setup_inputs(seed: int = 0) -> dict:
    streams_of = jax.random.split(jax.random.key(seed), 8)
    return {
        "hidden": draw_hidden(jax.random.fold_in(streams_of[7], 71), 0),
        "norm_gain": jnp.clip(1.0 + 0.18 * jax.random.normal(streams_of[1], (D,), jnp.float32), 0.1, 1.9),
        "w_query": gaussian(streams_of[2], (D, QH * HD), (D // 7) ** -0.5, 0.25, ((1, 4),)),
        "w_key": gaussian(streams_of[3], (D, KVH * HD), D ** -0.5, 0.09375, ((1, 4),)),
        "w_value": gaussian(streams_of[4], (D, KVH * HD), D ** -0.5, 0.09375, ((1, 4),)),
        "segment_ids": draw_segment_ids(jax.random.fold_in(streams_of[7], 71), 0),
        "page_table": jax.vmap(lambda own: jax.random.permutation(own, PAGES_DEV))(jax.random.split(streams_of[6], N_SEQ)).reshape((N_SEQ, PAGES_DEV)).astype(jnp.int32),
    }


logit_cap = 50.0
query_scale = 144.0 ** (-0.5)
norm_eps = 1e-06

def rotate(heads, positions):
    half_dim = HD // 2
    freqs = 10000.0 ** (-(jnp.arange(half_dim, dtype=jnp.float32) * (2.0 / HD)))
    angles = positions.astype(jnp.float32)[:, None] * freqs[None, :]
    cosine = jnp.cos(angles)[:, None, :]
    sine_part = jnp.sin(angles)[:, None, :]
    first_half = heads[..., :half_dim]
    second_half = heads[..., half_dim:]
    return jnp.concatenate([first_half * cosine - second_half * sine_part, second_half * cosine + first_half * sine_part], axis=-1)

def reference(hidden, norm_gain, w_query, w_key, w_value, segment_ids, page_table):
    wide = hidden.astype(jnp.float32)
    meansq = lax.optimization_barrier(jnp.mean(wide * wide, axis=-1, keepdims=True))
    normed = (wide * lax.rsqrt(meansq + norm_eps) * norm_gain).astype(jnp.bfloat16)
    queries_raw = jnp.dot(normed, w_query, preferred_element_type=jnp.float32)
    keys_raw = jnp.dot(normed, w_key, preferred_element_type=jnp.float32)
    values = jnp.dot(normed, w_value, preferred_element_type=jnp.float32).astype(jnp.bfloat16)
    index_all = jnp.arange(STREAM, dtype=jnp.int32)
    earlier = jnp.concatenate([jnp.full((1,), -1, jnp.int32), segment_ids[:-1].astype(jnp.int32)])
    marks = jnp.where(segment_ids != earlier, index_all, 0).astype(jnp.int32)
    starts = lax.cummax(marks, axis=0)
    positions = index_all - starts
    queries = rotate(queries_raw.reshape(STREAM, QH, HD), positions).astype(jnp.bfloat16)
    queries = queries.reshape(STREAM, KVH, QH // KVH, HD)
    keys = rotate(keys_raw.reshape(STREAM, KVH, HD), positions).astype(jnp.bfloat16)
    value_heads = values.reshape(STREAM, KVH, HD)
    pad_keys = jnp.concatenate([jnp.zeros((WIN, KVH, HD), jnp.bfloat16), keys], axis=0)
    pad_values = jnp.concatenate([jnp.zeros((WIN, KVH, HD), jnp.bfloat16), value_heads], axis=0)

    def one_block(block_id):
        first = (block_id * TOK_DEV).astype(jnp.int32)
        query_block = lax.dynamic_slice_in_dim(queries, first, TOK_DEV, 0).astype(jnp.float32)
        key_block = lax.dynamic_slice_in_dim(pad_keys, first, WIN + TOK_DEV, 0).astype(jnp.float32)
        value_block = lax.dynamic_slice_in_dim(pad_values, first, WIN + TOK_DEV, 0).astype(jnp.float32)
        start_block = lax.dynamic_slice_in_dim(starts, first, TOK_DEV, 0)
        query_index = first + jnp.arange(TOK_DEV, dtype=jnp.int32)
        key_index = first - WIN + jnp.arange(WIN + TOK_DEV, dtype=jnp.int32)
        scores = jnp.einsum('qgrd,kgd->grqk', query_block, key_block) * query_scale
        capped = logit_cap * jnp.tanh(scores / logit_cap)
        allowed = (key_index[None, :] >= start_block[:, None]) & (key_index[None, :] <= query_index[:, None]) & (query_index[:, None] - key_index[None, :] < WIN)
        weights = jnp.where(allowed, jnp.exp(capped), 0.0)
        totals = lax.optimization_barrier(jnp.sum(weights, axis=-1))
        rounded = lax.optimization_barrier(weights.astype(jnp.bfloat16)).astype(jnp.float32)
        numerator = jnp.einsum('grqk,kgd->grqd', rounded, value_block)
        mixed = numerator / totals[..., None]
        return jnp.transpose(mixed, (2, 0, 1, 3)).reshape(TOK_DEV, QH * HD).astype(jnp.bfloat16)
    attended = lax.map(one_block, jnp.arange(STREAM // TOK_DEV, dtype=jnp.int32)).reshape(STREAM, QH * HD)
    stacked = jnp.stack([keys.reshape(STREAM, KVH * HD), values], axis=1).reshape(NPAGES, PAGE, 2, KVH * HD)
    page_ids = jnp.arange(NPAGES, dtype=jnp.int32)
    targets = page_ids // PAGES_DEV * PAGES_DEV + page_table.reshape(NPAGES).astype(jnp.int32)
    kv_cache = jnp.zeros_like(stacked).at[targets].set(stacked)
    return (attended, kv_cache)
```

```python
import functools
import math

import jax
import jax.numpy as jnp
from jax import lax
from jax.experimental import pallas as pl
from jax.experimental.pallas import tpu as pltpu
from jax.sharding import PartitionSpec as P

HD = 128
WIN = 4096
PAGE = 128
MESH = pl.DeviceIdType.MESH

logit_cap = 50.0
query_scale = 144.0 ** (-0.5)
norm_eps = 1e-06
SCORE_IN = query_scale / logit_cap
SCORE_OUT = logit_cap * math.log2(math.e)


def layer_kernel(
    n, back, hops, chunks,
    hidden, gain, w_query, w_key, w_value, ids_row, ids_col, freqs, table,
    attended, cache,
    hid, weights, normed, queries, own, line, pair, ids_all, numer, totals, staged, landed,
    local_sem, hid_send, hid_recv, line_send, line_recv, pair_send, pair_recv,
    ids_send, ids_recv, cache_send, cache_recv,
):
    tokens, width = hidden.shape
    model = gain.shape[1]
    q_cols, kv_cols = w_query.shape[1], w_key.shape[1]
    kv_heads = kv_cols // HD
    repeat = q_cols // kv_cols
    rows_in = tokens // chunks
    place, t = lax.axis_index("seq"), lax.axis_index("tp")
    side = place % 2
    rank = place // 2
    ranks = n // 2
    mate = place + 1 - 2 * side
    t1 = t + 1 - 2 * (t % 2)
    t2 = (t + 2) % 4
    t3 = (t1 + 2) % 4

    def rows_of(c):
        return pl.ds(pl.multiple_of(c * rows_in, rows_in), rows_in)

    def cols_of(k):
        return pl.ds(pl.multiple_of(k * width, 128), width)

    def remote(src, dst, send, recv, where):
        return pltpu.make_async_remote_copy(
            src_ref=src, dst_ref=dst, send_sem=send, recv_sem=recv,
            device_id=where, device_id_type=MESH,
        )

    loads = [
        pltpu.make_async_copy(w_query, weights.at[:, pl.ds(0, q_cols)], local_sem.at[0]),
        pltpu.make_async_copy(w_key, weights.at[:, pl.ds(q_cols, kv_cols)], local_sem.at[1]),
        pltpu.make_async_copy(
            w_value, weights.at[:, pl.ds(q_cols + kv_cols, kv_cols)], local_sem.at[2]
        ),
        pltpu.make_async_copy(hidden, hid.at[:, cols_of(t)], local_sem.at[3]),
    ]
    for load in loads:
        load.start()
    ids_all[...] = jnp.full_like(ids_all, -1)

    barrier = pltpu.get_barrier_semaphore()
    for d in range(1, back + 1):
        for other, there in ((place + d, place + d < n), (place - d, place >= d)):
            @pl.when(there)
            def _():
                pl.semaphore_signal(barrier, 1, device_id=(other, t), device_id_type=MESH)
    for k in range(1, 4):
        pl.semaphore_signal(barrier, 1, device_id=(place, (t + k) % 4), device_id_type=MESH)
    peers = 3
    for d in range(1, back + 1):
        peers = peers + jnp.where(place + d < n, 1, 0) + jnp.where(place >= d, 1, 0)
    pl.semaphore_wait(barrier, peers)

    def hid_copy(stream, c):
        rows = rows_of(c)
        if stream == 0:
            src, dst, to = hidden.at[rows], hid.at[rows, cols_of(t)], t1
        elif stream == 1:
            src, dst, to = hidden.at[rows], hid.at[rows, cols_of(t)], t2
        else:
            src, dst, to = hid.at[rows, cols_of(t2)], hid.at[rows, cols_of(t2)], t1
        return remote(src, dst, hid_send.at[stream, c], hid_recv.at[stream, c], (place, to))

    def hid_arrival(stream, c):
        rows = rows_of(c)
        dst = hid.at[rows, cols_of((t1, t2, t3)[stream])]
        return remote(dst, dst, hid_send.at[stream, c], hid_recv.at[stream, c], (place, t1))

    def ids_copy(d):
        return remote(
            ids_row, ids_all.at[d - 1], ids_send.at[d - 1], ids_recv.at[d - 1], (place + d, t)
        )

    for d in range(1, back + 1):
        @pl.when(place + d < n)
        def _():
            ids_copy(d).start()

    def first_sends(c, carry):
        hid_copy(1, c).start()
        hid_copy(0, c).start()
        return carry

    lax.fori_loop(0, chunks, first_sends, 0)

    def block_at(h, c):
        return own.at[rows_of(c)] if h == 0 else line.at[h - 1, rows_of(c)]

    def line_copy(h, c):
        return remote(
            block_at(h, c), line.at[h, rows_of(c)],
            line_send.at[h, c], line_recv.at[h, c], (place + 2, t),
        )

    def line_goes(h):
        return (rank >= h) & (rank + 1 < ranks)

    def pair_copy(h, c):
        return remote(
            block_at(h, c), pair.at[h, rows_of(c)],
            pair_send.at[h, c], pair_recv.at[h, c], (mate, t),
        )

    def pair_goes(h, at):
        reach = 2 * h + 1 - 2 * at
        return (rank >= h) & (reach > 0) & (reach <= back)

    def pass_on(h, c):
        if h < hops:
            @pl.when(line_goes(h))
            def _():
                line_copy(h, c).start()

        @pl.when(pair_goes(h, side))
        def _():
            pair_copy(h, c).start()

    def forward(h, c):
        @pl.when(rank >= h)
        def _():
            block = line.at[h - 1, rows_of(c)]
            remote(
                block, block, line_send.at[h - 1, c], line_recv.at[h - 1, c], (place, t1)
            ).wait_recv()
            pass_on(h, c)

    for d in range(1, back + 1):
        @pl.when(place >= d)
        def _():
            here = ids_all.at[d - 1]
            remote(here, here, ids_send.at[d - 1], ids_recv.at[d - 1], (place, t1)).wait_recv()

    first_id = ids_col[0:1, 0:1]
    prior = jnp.zeros((1, 1), jnp.float32)
    for d in range(back):
        same = jnp.where(ids_all[d, 0:1, :] == first_id, 1.0, 0.0)
        prior = prior + jnp.sum(same, axis=1, keepdims=True)

    for load in loads:
        load.wait()
    numer[...] = jnp.zeros_like(numer)
    totals[...] = jnp.zeros_like(totals)

    def project(c, carry):
        rows = rows_of(c)
        hid_arrival(1, c).wait_recv()
        hid_copy(2, c).start()
        ids_here = ids_col[rows, :]
        wide_ids = jnp.concatenate([ids_here] * (tokens // 128), axis=1)
        shape = (rows_in, tokens)
        earlier = lax.broadcasted_iota(jnp.int32, shape, 1) < (
            lax.broadcasted_iota(jnp.int32, shape, 0) + c * rows_in
        )
        local = jnp.where((wide_ids == ids_row[0:1, :]) & earlier, 1.0, 0.0)
        positions = jnp.sum(local, axis=1, keepdims=True) + jnp.where(
            ids_here == first_id, prior, 0.0
        )
        angles = positions * freqs[0:1, :]
        cosine = jnp.cos(angles)
        sine = jnp.sin(angles)
        sine = jnp.where(
            lax.broadcasted_iota(jnp.int32, sine.shape, 1) < HD // 2, -sine, sine
        )
        hid_arrival(0, c).wait_recv()
        hid_arrival(2, c).wait_recv()
        parts = model // width
        squares = jnp.zeros((rows_in, 1), jnp.float32)
        for k in range(parts):
            piece = hid[rows, k * width:(k + 1) * width].astype(jnp.float32)
            squares = squares + jnp.sum(piece * piece, axis=1, keepdims=True)
        scale = lax.rsqrt(squares * (1.0 / model) + norm_eps)
        for k in range(parts):
            here = slice(k * width, (k + 1) * width)
            piece = hid[rows, here].astype(jnp.float32)
            normed[:, here] = (piece * scale * gain[0:1, here]).astype(jnp.bfloat16)
        raw = jnp.dot(normed[...], weights[...], preferred_element_type=jnp.float32)

        def rotated(x):
            return (x * cosine + pltpu.roll(x, HD // 2, 1) * sine).astype(jnp.bfloat16)

        for j in range(kv_heads):
            at = q_cols + j * HD
            own[rows, j * HD:(j + 1) * HD] = rotated(raw[:, at:at + HD])
        own[rows, kv_cols:] = raw[:, q_cols + kv_cols:].astype(jnp.bfloat16)
        pass_on(0, c)
        for j in range(q_cols // HD):
            queries[j, rows, :] = rotated(raw[:, j * HD:(j + 1) * HD])
        for h in range(1, hops + 1):
            @pl.when(c >= h)
            def _():
                forward(h, c - h)
        return carry

    lax.fori_loop(0, chunks, project, 0)

    tile = min(256, tokens)

    def attend(block, id_row, causal):
        def one(step, carry):
            group, at = step // (tokens // tile), step % (tokens // tile)
            rows = pl.ds(pl.multiple_of(at * tile, tile), tile)
            keys = block[:, pl.ds(pl.multiple_of(group * HD, HD), HD)]
            values = block[:, pl.ds(pl.multiple_of(kv_cols + group * HD, HD), HD)]
            allowed = jnp.concatenate([ids_col[rows, :]] * (tokens // 128), axis=1) == id_row
            if causal:
                shape = (tile, tokens)
                allowed = allowed & (
                    lax.broadcasted_iota(jnp.int32, shape, 1)
                    <= lax.broadcasted_iota(jnp.int32, shape, 0) + at * tile
                )
            for k in range(repeat):
                head = group * repeat + k
                scores = lax.dot_general(
                    queries[head, rows, :], keys, (((1,), (1,)), ((), ())),
                    preferred_element_type=jnp.float32,
                )
                raised = jnp.exp2(SCORE_OUT * jnp.tanh(scores * SCORE_IN))
                wts = jnp.where(allowed, raised, 0.0)
                part = wts[:, :128]
                for m in range(1, tokens // 128):
                    part = part + wts[:, m * 128:(m + 1) * 128]
                totals[head, rows, :] += part
                numer[head, rows, :] += jnp.dot(
                    wts.astype(jnp.bfloat16), values, preferred_element_type=jnp.float32
                )
            return carry

        lax.fori_loop(0, kv_heads * (tokens // tile), one, 0)

    def attend_line(h):
        if 2 * h > back:
            return

        @pl.when(rank >= h)
        def _():
            attend(line.at[h - 1], ids_all[2 * h - 1, 0:1, :], False)

    def attend_pair(h):
        @pl.when(pair_goes(h, 1 - side))
        def _():
            for c in range(chunks):
                block = pair.at[h, rows_of(c)]
                remote(
                    block, block, pair_send.at[h, c], pair_recv.at[h, c], (place, t1)
                ).wait_recv()
            attend(pair.at[h], ids_all[2 * h + 2 * side - 2, 0:1, :], False)

    for j in range(chunks):
        picked = own[0:rows_in, :]
        for g in range(1, chunks):
            picked = jnp.where(table[0, g] == j, own[g * rows_in:(g + 1) * rows_in, :], picked)
        staged[j] = picked

        @pl.when(t == j)
        def _():
            landed[j] = picked

    def cache_copy(k):
        j = (t + k) % 4
        return remote(
            staged.at[j], landed.at[t], cache_send.at[k], cache_recv.at[k], (place, j)
        )

    for k in range(1, 4):
        cache_copy(k).start()

    attend(own, ids_row[0:1, :], True)
    for h in range(1, hops + 1):
        for later in range(h, hops + 1):
            for c in range(chunks):
                if c + later == chunks - 1 + h:
                    forward(later, c)
        attend_pair(h - 1)
        attend_line(h)
    attend_pair(hops)

    for head in range(q_cols // HD):
        total = jnp.sum(totals[head], axis=1, keepdims=True)
        attended[:, head * HD:(head + 1) * HD] = (numer[head] / total).astype(jnp.bfloat16)

    for k in range(1, 4):
        cache_copy(k).wait_send()
        got = landed.at[(t + 4 - k) % 4]
        remote(got, got, cache_send.at[k], cache_recv.at[k], (place, t1)).wait_recv()
    cache[...] = landed[...]

    def drain(c, carry):
        for stream in range(3):
            hid_copy(stream, c).wait_send()
        for h in range(hops + 1):
            if h < hops:
                @pl.when(line_goes(h))
                def _():
                    line_copy(h, c).wait_send()

            @pl.when(pair_goes(h, side))
            def _():
                pair_copy(h, c).wait_send()
        return carry

    lax.fori_loop(0, chunks, drain, 0)
    for d in range(1, back + 1):
        @pl.when(place + d < n)
        def _():
            ids_copy(d).wait_send()


def per_device(n, hidden, norm_gain, w_query, w_key, w_value, segment_ids, page_table):
    tokens, width = hidden.shape
    model = norm_gain.shape[0]
    q_cols, kv_cols = w_query.shape[1], w_key.shape[1]
    chunks = tokens // PAGE
    back = min(WIN // tokens, n - 1)
    hops = min(n // 2 - 1, (back + 1) // 2)
    ids_row = jnp.broadcast_to(segment_ids[None, :], (8, tokens))
    ids_col = jnp.broadcast_to(segment_ids[:, None], (tokens, 128))
    half = HD // 2
    freqs = 10000.0 ** (-(jnp.arange(half, dtype=jnp.float32) * (2.0 / HD)))
    freqs = jnp.broadcast_to(jnp.concatenate([freqs, freqs])[None, :], (8, HD))
    vmem = pl.BlockSpec(memory_space=pltpu.VMEM)
    hbm = pl.BlockSpec(memory_space=pl.ANY)
    heads = q_cols // HD
    dma = pltpu.SemaphoreType.DMA
    attended, cache = pl.pallas_call(
        functools.partial(layer_kernel, n, back, hops, chunks),
        out_shape=(
            jax.ShapeDtypeStruct((tokens, q_cols), jnp.bfloat16),
            jax.ShapeDtypeStruct((chunks, PAGE, 2 * kv_cols), jnp.bfloat16),
        ),
        in_specs=[
            vmem, vmem, hbm, hbm, hbm, vmem, vmem, vmem,
            pl.BlockSpec(memory_space=pltpu.SMEM),
        ],
        out_specs=(vmem, vmem),
        scratch_shapes=[
            pltpu.VMEM((tokens, model), jnp.bfloat16),
            pltpu.VMEM((model, q_cols + 2 * kv_cols), jnp.bfloat16),
            pltpu.VMEM((tokens // chunks, model), jnp.bfloat16),
            pltpu.VMEM((heads, tokens, HD), jnp.bfloat16),
            pltpu.VMEM((tokens, 2 * kv_cols), jnp.bfloat16),
            pltpu.VMEM((hops, tokens, 2 * kv_cols), jnp.bfloat16),
            pltpu.VMEM((hops + 1, tokens, 2 * kv_cols), jnp.bfloat16),
            pltpu.VMEM((back, 8, tokens), jnp.int32),
            pltpu.VMEM((heads, tokens, HD), jnp.float32),
            pltpu.VMEM((heads, tokens, 128), jnp.float32),
            pltpu.VMEM((chunks, PAGE, 2 * kv_cols), jnp.bfloat16),
            pltpu.VMEM((chunks, PAGE, 2 * kv_cols), jnp.bfloat16),
            dma((4,)),
            dma((3, chunks)), dma((3, chunks)),
            dma((hops, chunks)), dma((hops, chunks)),
            dma((hops + 1, chunks)), dma((hops + 1, chunks)),
            dma((back,)), dma((back,)),
            dma((4,)), dma((4,)),
        ],
        compiler_params=pltpu.CompilerParams(
            collective_id=0, has_side_effects=True, vmem_limit_bytes=56 * 1024 * 1024
        ),
        cost_estimate=pl.CostEstimate(
            flops=2 * tokens * model * (q_cols + 2 * kv_cols)
            + 4 * heads * tokens * HD * tokens * (back + 1),
            bytes_accessed=2 * model * (q_cols + 2 * kv_cols),
            transcendentals=2 * heads * tokens * tokens * (back + 1),
        ),
    )(
        hidden, norm_gain[None, :], w_query, w_key, w_value, ids_row, ids_col, freqs, page_table
    )
    pages = cache.reshape(chunks, PAGE, 2, kv_cols)
    kv_cache = jnp.transpose(pages, (1, 2, 0, 3)).reshape(1, PAGE, 2, chunks * kv_cols)
    return (attended, kv_cache)


def solution(mesh):
    placed = (
        P("seq", "tp"),
        P(),
        P(None, "tp"),
        P(None, "tp"),
        P(None, "tp"),
        P("seq"),
        P("seq", None),
    )
    return jax.shard_map(
        functools.partial(per_device, mesh.shape["seq"]),
        mesh=mesh,
        in_specs=placed,
        out_specs=(P("seq", "tp"), P(("seq", "tp"), None, None, None)),
        check_vma=False,
    )
```

```python
import functools
import math

import jax
import jax.numpy as jnp
import numpy as np
from jax import lax
from jax.experimental import pallas as pl
from jax.experimental.pallas import tpu as pltpu
from jax.sharding import PartitionSpec as P

HD = 128
WIN = 4096
PAGE = 128
MESH = pl.DeviceIdType.MESH

logit_cap = 50.0
query_scale = 144.0 ** (-0.5)
norm_eps = 1e-06
SCORE_IN = query_scale / logit_cap
SCORE_OUT = logit_cap * math.log2(math.e)


def layer_kernel(
    n, back, hops, chunks,
    hidden, gain_flat, w_query, w_key, w_value, ids_flat, freqs, table,
    attended, cache,
    gain, ids_row, ids_col, cosines, sines, woven,
    hid, weights, normed, queries, own, line, pair, ids_all, numer, totals, staged, landed,
    local_sem, hid_send, hid_recv, line_send, line_recv, pair_send, pair_recv,
    ids_send, ids_recv, cache_send, cache_recv,
):
    tokens, width = hidden.shape
    model = gain.shape[1]
    q_cols, kv_cols = w_query.shape[1], w_key.shape[1]
    kv_heads = kv_cols // HD
    repeat = q_cols // kv_cols
    rows_in = tokens // chunks
    place, t = lax.axis_index("seq"), lax.axis_index("tp")
    side = place % 2
    rank = place // 2
    ranks = n // 2
    mate = place + 1 - 2 * side
    t1 = t + 1 - 2 * (t % 2)
    t2 = (t + 2) % 4
    t3 = (t1 + 2) % 4

    def rows_of(c):
        return pl.ds(pl.multiple_of(c * rows_in, rows_in), rows_in)

    def cols_of(k):
        return pl.ds(pl.multiple_of(k * width, 128), width)

    def remote(src, dst, send, recv, where):
        return pltpu.make_async_remote_copy(
            src_ref=src, dst_ref=dst, send_sem=send, recv_sem=recv,
            device_id=where, device_id_type=MESH,
        )

    loads = [
        pltpu.make_async_copy(w_query, weights.at[:, pl.ds(0, q_cols)], local_sem.at[0]),
        pltpu.make_async_copy(w_key, weights.at[:, pl.ds(q_cols, kv_cols)], local_sem.at[1]),
        pltpu.make_async_copy(
            w_value, weights.at[:, pl.ds(q_cols + kv_cols, kv_cols)], local_sem.at[2]
        ),
        pltpu.make_async_copy(hidden, hid.at[:, cols_of(t)], local_sem.at[3]),
    ]
    for load in loads:
        load.start()
    ids_all[...] = jnp.full_like(ids_all, -1)
    ids_row[...] = jnp.broadcast_to(ids_flat[...].reshape(1, tokens), (8, tokens))

    barrier = pltpu.get_barrier_semaphore()
    for d in range(1, back + 1):
        for other, there in ((place + d, place + d < n), (place - d, place >= d)):
            @pl.when(there)
            def _():
                pl.semaphore_signal(barrier, 1, device_id=(other, t), device_id_type=MESH)
    for k in range(1, 4):
        pl.semaphore_signal(barrier, 1, device_id=(place, (t + k) % 4), device_id_type=MESH)
    peers = 3
    for d in range(1, back + 1):
        peers = peers + jnp.where(place + d < n, 1, 0) + jnp.where(place >= d, 1, 0)
    pl.semaphore_wait(barrier, peers)

    def hid_copy(stream, c):
        rows = rows_of(c)
        if stream == 0:
            src, dst, to = hidden.at[rows], hid.at[rows, cols_of(t)], t1
        elif stream == 1:
            src, dst, to = hidden.at[rows], hid.at[rows, cols_of(t)], t2
        else:
            src, dst, to = hid.at[rows, cols_of(t2)], hid.at[rows, cols_of(t2)], t1
        return remote(src, dst, hid_send.at[stream, c], hid_recv.at[stream, c], (place, to))

    def hid_arrival(stream, c):
        rows = rows_of(c)
        dst = hid.at[rows, cols_of((t1, t2, t3)[stream])]
        return remote(dst, dst, hid_send.at[stream, c], hid_recv.at[stream, c], (place, t1))

    def ids_copy(d):
        return remote(
            ids_row, ids_all.at[d - 1], ids_send.at[d - 1], ids_recv.at[d - 1], (place + d, t)
        )

    for d in range(1, back + 1):
        @pl.when(place + d < n)
        def _():
            ids_copy(d).start()

    def first_sends(c, carry):
        hid_copy(1, c).start()
        hid_copy(0, c).start()
        return carry

    lax.fori_loop(0, chunks, first_sends, 0)

    def block_at(h, c):
        return own.at[rows_of(c)] if h == 0 else line.at[h - 1, rows_of(c)]

    def line_copy(h, c):
        return remote(
            block_at(h, c), line.at[h, rows_of(c)],
            line_send.at[h, c], line_recv.at[h, c], (place + 2, t),
        )

    def line_goes(h):
        return (rank >= h) & (rank + 1 < ranks)

    def pair_copy(h, c):
        return remote(
            block_at(h, c), pair.at[h, rows_of(c)],
            pair_send.at[h, c], pair_recv.at[h, c], (mate, t),
        )

    def pair_goes(h, at):
        reach = 2 * h + 1 - 2 * at
        return (rank >= h) & (reach > 0) & (reach <= back)

    def pass_on(h, c):
        if h < hops:
            @pl.when(line_goes(h))
            def _():
                line_copy(h, c).start()

        @pl.when(pair_goes(h, side))
        def _():
            pair_copy(h, c).start()

    def forward(h, c):
        @pl.when(rank >= h)
        def _():
            block = line.at[h - 1, rows_of(c)]
            remote(
                block, block, line_send.at[h - 1, c], line_recv.at[h - 1, c], (place, t1)
            ).wait_recv()
            pass_on(h, c)

    for d in range(1, back + 1):
        @pl.when(place >= d)
        def _():
            here = ids_all.at[d - 1]
            remote(here, here, ids_send.at[d - 1], ids_recv.at[d - 1], (place, t1)).wait_recv()

    gain[...] = jnp.broadcast_to(gain_flat[...].reshape(1, model), gain.shape)
    for c in range(tokens // 128):
        here = slice(c * 128, (c + 1) * 128)
        spread = jnp.broadcast_to(ids_row[0:1, here].astype(jnp.float32), (128, 128))
        ids_col[here, :] = jnp.transpose(spread).astype(jnp.int32)
    first_id = ids_col[0:1, 0:1]
    prior = jnp.zeros((1, 1), jnp.float32)
    for d in range(back):
        same = jnp.where(ids_all[d, 0:1, :] == first_id, 1.0, 0.0)
        prior = prior + jnp.sum(same, axis=1, keepdims=True)

    def prepare(c, carry):
        rows = rows_of(c)
        ids_here = ids_col[rows, :]
        wide_ids = jnp.concatenate([ids_here] * (tokens // 128), axis=1)
        shape = (rows_in, tokens)
        earlier = lax.broadcasted_iota(jnp.int32, shape, 1) < (
            lax.broadcasted_iota(jnp.int32, shape, 0) + c * rows_in
        )
        local = jnp.where((wide_ids == ids_row[0:1, :]) & earlier, 1.0, 0.0)
        positions = jnp.sum(local, axis=1, keepdims=True) + jnp.where(
            ids_here == first_id, prior, 0.0
        )
        angles = positions * freqs[0:1, :]
        sine = jnp.sin(angles)
        cosines[rows, :] = jnp.cos(angles)
        sines[rows, :] = jnp.where(
            lax.broadcasted_iota(jnp.int32, sine.shape, 1) < HD // 2, -sine, sine
        )
        return carry

    lax.fori_loop(0, chunks, prepare, 0)
    numer[...] = jnp.zeros_like(numer)
    totals[...] = jnp.zeros_like(totals)
    own[...] = jnp.zeros_like(own)
    for load in loads:
        load.wait()

    def attend_tile(block, id_row, group, at, size, causal):
        rows = pl.ds(pl.multiple_of(at * size, size), size)
        keys = block[:, pl.ds(pl.multiple_of(group * HD, HD), HD)]
        values = block[:, pl.ds(pl.multiple_of(kv_cols + group * HD, HD), HD)]
        allowed = jnp.concatenate([ids_col[rows, :]] * (tokens // 128), axis=1) == id_row
        if causal:
            shape = (size, tokens)
            allowed = allowed & (
                lax.broadcasted_iota(jnp.int32, shape, 1)
                <= lax.broadcasted_iota(jnp.int32, shape, 0) + at * size
            )
        for k in range(repeat):
            head = group * repeat + k
            scores = lax.dot_general(
                queries[head, rows, :], keys, (((1,), (1,)), ((), ())),
                preferred_element_type=jnp.float32,
            )
            raised = jnp.exp2(SCORE_OUT * jnp.tanh(scores * SCORE_IN))
            wts = jnp.where(allowed, raised, 0.0)
            part = wts[:, :128]
            for m in range(1, tokens // 128):
                part = part + wts[:, m * 128:(m + 1) * 128]
            totals[head, rows, :] += part
            numer[head, rows, :] += jnp.dot(
                wts.astype(jnp.bfloat16), values, preferred_element_type=jnp.float32
            )

    def project(c, carry):
        rows = rows_of(c)
        hid_arrival(1, c).wait_recv()
        hid_copy(2, c).start()
        hid_arrival(0, c).wait_recv()
        squares = jnp.zeros((rows_in, 1), jnp.float32)
        for k in (t, t1, t2, t3):
            if k is t3:
                hid_arrival(2, c).wait_recv()
            piece = hid[rows, cols_of(k)].astype(jnp.float32)
            squares = squares + jnp.sum(piece * piece, axis=1, keepdims=True)
        scale = lax.rsqrt(squares * (1.0 / model) + norm_eps)
        for k in range(model // width):
            here = slice(k * width, (k + 1) * width)
            piece = hid[rows, here].astype(jnp.float32)
            normed[:, here] = (piece * scale * gain[0:1, here]).astype(jnp.bfloat16)
        raw = jnp.dot(normed[...], weights[...], preferred_element_type=jnp.float32)
        cosine, sine = cosines[rows, :], sines[rows, :]

        def rotated(x):
            return (x * cosine + pltpu.roll(x, HD // 2, 1) * sine).astype(jnp.bfloat16)

        for j in range(kv_heads):
            at = q_cols + j * HD
            own[rows, j * HD:(j + 1) * HD] = rotated(raw[:, at:at + HD])
        own[rows, kv_cols:] = raw[:, q_cols + kv_cols:].astype(jnp.bfloat16)
        pass_on(0, c)
        for j in range(q_cols // HD):
            queries[j, rows, :] = rotated(raw[:, j * HD:(j + 1) * HD])
        for group in range(kv_heads):
            attend_tile(own, ids_row[0:1, :], group, c, rows_in, True)
        for h in range(1, hops + 1):
            @pl.when(c >= h)
            def _():
                forward(h, c - h)
        return carry

    lax.fori_loop(0, chunks, project, 0)

    tile = min(256, tokens)

    def attend(block, id_row):
        def one(step, carry):
            group, at = step // (tokens // tile), step % (tokens // tile)
            attend_tile(block, id_row, group, at, tile, False)
            return carry

        lax.fori_loop(0, kv_heads * (tokens // tile), one, 0)

    def attend_line(h):
        if 2 * h > back:
            return

        @pl.when(rank >= h)
        def _():
            attend(line.at[h - 1], ids_all[2 * h - 1, 0:1, :])

    def attend_pair(h):
        @pl.when(pair_goes(h, 1 - side))
        def _():
            for c in range(chunks):
                block = pair.at[h, rows_of(c)]
                remote(
                    block, block, pair_send.at[h, c], pair_recv.at[h, c], (place, t1)
                ).wait_recv()
            attend(pair.at[h], ids_all[2 * h + 2 * side - 2, 0:1, :])

    for j in range(chunks):
        picked = own[0:rows_in, :]
        for g in range(1, chunks):
            picked = jnp.where(table[0, g] == j, own[g * rows_in:(g + 1) * rows_in, :], picked)
        staged[j] = picked

        @pl.when(t == j)
        def _():
            landed[j] = picked

    def cache_copy(k):
        j = (t + k) % 4
        return remote(
            staged.at[j], landed.at[t], cache_send.at[k], cache_recv.at[k], (place, j)
        )

    for k in range(1, 4):
        cache_copy(k).start()

    waiting = [("pair", 0)]
    for h in range(1, hops + 1):
        waiting += [("line", h), ("pair", h)]
    ready = 0
    for h in range(1, hops + 1):
        for later in range(h, hops + 1):
            forward(later, chunks - 1 + h - later)
        kind, index = waiting[ready]
        (attend_pair if kind == "pair" else attend_line)(index)
        ready += 1
    for kind, index in waiting[ready:]:
        (attend_pair if kind == "pair" else attend_line)(index)

    for head in range(q_cols // HD):
        total = jnp.sum(totals[head], axis=1, keepdims=True)
        attended[:, head * HD:(head + 1) * HD] = (numer[head] / total).astype(jnp.bfloat16)

    for k in range(1, 4):
        cache_copy(k).wait_send()
        got = landed.at[(t + 4 - k) % 4]
        remote(got, got, cache_send.at[k], cache_recv.at[k], (place, t1)).wait_recv()
    for k in range(chunks):
        for part in range(2):
            got = landed[k, :, part * kv_cols:(part + 1) * kv_cols].astype(jnp.float32)
            for m in range(kv_cols // 128):
                at = k * (kv_cols // 128) + m
                woven[at, pl.ds(part, PAGE, stride=2), :] = got[:, m * 128:(m + 1) * 128]
    for at in range(chunks * kv_cols // 128):
        cache[:, at * 128:(at + 1) * 128] = woven[at].astype(jnp.bfloat16)

    def drain(c, carry):
        for stream in range(3):
            hid_copy(stream, c).wait_send()
        for h in range(hops + 1):
            if h < hops:
                @pl.when(line_goes(h))
                def _():
                    line_copy(h, c).wait_send()

            @pl.when(pair_goes(h, side))
            def _():
                pair_copy(h, c).wait_send()
        return carry

    lax.fori_loop(0, chunks, drain, 0)
    for d in range(1, back + 1):
        @pl.when(place + d < n)
        def _():
            ids_copy(d).wait_send()


def per_device(n, hidden, norm_gain, w_query, w_key, w_value, segment_ids, page_table):
    tokens, width = hidden.shape
    model = norm_gain.shape[0]
    q_cols, kv_cols = w_query.shape[1], w_key.shape[1]
    chunks = tokens // PAGE
    back = min(WIN // tokens, n - 1)
    hops = min(n // 2 - 1, (back + 1) // 2)
    half = HD // 2
    freqs = np.power(np.float32(10000.0), -(np.arange(half, dtype=np.float32) * np.float32(2.0 / HD)))
    freqs = np.tile(np.concatenate([freqs, freqs])[None, :], (8, 1)).astype(np.float32)
    vmem = pl.BlockSpec(memory_space=pltpu.VMEM)
    hbm = pl.BlockSpec(memory_space=pl.ANY)
    heads = q_cols // HD
    dma = pltpu.SemaphoreType.DMA
    attended, cache = pl.pallas_call(
        functools.partial(layer_kernel, n, back, hops, chunks),
        out_shape=(
            jax.ShapeDtypeStruct((tokens, q_cols), jnp.bfloat16),
            jax.ShapeDtypeStruct((2 * PAGE, chunks * kv_cols), jnp.bfloat16),
        ),
        in_specs=[
            vmem, vmem, hbm, hbm, hbm, vmem, vmem,
            pl.BlockSpec(memory_space=pltpu.SMEM),
        ],
        out_specs=(vmem, vmem),
        scratch_shapes=[
            pltpu.VMEM((8, model), jnp.float32),
            pltpu.VMEM((8, tokens), jnp.int32),
            pltpu.VMEM((tokens, 128), jnp.int32),
            pltpu.VMEM((tokens, HD), jnp.float32),
            pltpu.VMEM((tokens, HD), jnp.float32),
            pltpu.VMEM((chunks * kv_cols // 128, 2 * PAGE, 128), jnp.float32),
            pltpu.VMEM((tokens, model), jnp.bfloat16),
            pltpu.VMEM((model, q_cols + 2 * kv_cols), jnp.bfloat16),
            pltpu.VMEM((tokens // chunks, model), jnp.bfloat16),
            pltpu.VMEM((heads, tokens, HD), jnp.bfloat16),
            pltpu.VMEM((tokens, 2 * kv_cols), jnp.bfloat16),
            pltpu.VMEM((hops, tokens, 2 * kv_cols), jnp.bfloat16),
            pltpu.VMEM((hops + 1, tokens, 2 * kv_cols), jnp.bfloat16),
            pltpu.VMEM((back, 8, tokens), jnp.int32),
            pltpu.VMEM((heads, tokens, HD), jnp.float32),
            pltpu.VMEM((heads, tokens, 128), jnp.float32),
            pltpu.VMEM((chunks, PAGE, 2 * kv_cols), jnp.bfloat16),
            pltpu.VMEM((chunks, PAGE, 2 * kv_cols), jnp.bfloat16),
            dma((4,)),
            dma((3, chunks)), dma((3, chunks)),
            dma((hops, chunks)), dma((hops, chunks)),
            dma((hops + 1, chunks)), dma((hops + 1, chunks)),
            dma((back,)), dma((back,)),
            dma((4,)), dma((4,)),
        ],
        compiler_params=pltpu.CompilerParams(
            collective_id=0, has_side_effects=True, vmem_limit_bytes=56 * 1024 * 1024
        ),
        cost_estimate=pl.CostEstimate(
            flops=2 * tokens * model * (q_cols + 2 * kv_cols)
            + 4 * heads * tokens * HD * tokens * (back + 1),
            bytes_accessed=2 * model * (q_cols + 2 * kv_cols),
            transcendentals=2 * heads * tokens * tokens * (back + 1),
        ),
    )(
        hidden, norm_gain, w_query, w_key, w_value, segment_ids, freqs, page_table
    )
    kv_cache = cache.reshape(1, PAGE, 2, chunks * kv_cols)
    return (attended, kv_cache)


def solution(mesh):
    placed = (
        P("seq", "tp"),
        P(),
        P(None, "tp"),
        P(None, "tp"),
        P(None, "tp"),
        P("seq"),
        P("seq", None),
    )
    return jax.shard_map(
        functools.partial(per_device, mesh.shape["seq"]),
        mesh=mesh,
        in_specs=placed,
        out_specs=(P("seq", "tp"), P(("seq", "tp"), None, None, None)),
        check_vma=False,
    )
```

```python
import functools
import math

import jax
import jax.numpy as jnp
import numpy as np
from jax import lax
from jax.experimental import pallas as pl
from jax.experimental.pallas import tpu as pltpu
from jax.sharding import PartitionSpec as P

HD = 128
WIN = 4096
PAGE = 128
MESH = pl.DeviceIdType.MESH

logit_cap = 50.0
query_scale = 144.0 ** (-0.5)
norm_eps = 1e-06
CHUNKS = 4
SCORE_IN = query_scale / logit_cap
SCORE_OUT = logit_cap * math.log2(math.e)


def layer_kernel(
    n, back, hops, pages, chunks,
    hidden, gain_flat, w_query, w_key, w_value, ids_flat, freqs, table,
    attended, cache,
    gain, ids_row, ids_col, cosines, sines, woven, squares_own, squares_in, scales, raw_near, near,
    hid, weights, normed, queries, own, line, pair, ids_all, numer, totals, staged, landed,
    local_sem, hid_send, hid_recv, line_send, line_recv, pair_send, pair_recv,
    ids_send, ids_recv, cache_send, cache_recv, sq_send, sq_recv, relay_send,
):
    tokens, width = hidden.shape
    model = gain.shape[1]
    q_cols, kv_cols = w_query.shape[1], w_key.shape[1]
    kv_heads = kv_cols // HD
    repeat = q_cols // kv_cols
    rows_in = tokens // chunks
    half = 2 * width
    place, t = lax.axis_index("seq"), lax.axis_index("tp")
    side = place % 2
    rank = place // 2
    ranks = n // 2
    mate = place + 1 - 2 * side
    t1 = t + 1 - 2 * (t % 2)
    t2 = (t + 2) % 4
    t3 = (t1 + 2) % 4

    def rows_of(c):
        return pl.ds(pl.multiple_of(c * rows_in, rows_in), rows_in)

    def cols_of(k):
        return pl.ds(pl.multiple_of(k * width, 128), width)

    def remote(src, dst, send, recv, where):
        return pltpu.make_async_remote_copy(
            src_ref=src, dst_ref=dst, send_sem=send, recv_sem=recv,
            device_id=where, device_id_type=MESH,
        )

    loads = [
        pltpu.make_async_copy(w_query, weights.at[:, pl.ds(0, q_cols)], local_sem.at[0]),
        pltpu.make_async_copy(w_key, weights.at[:, pl.ds(q_cols, kv_cols)], local_sem.at[1]),
        pltpu.make_async_copy(
            w_value, weights.at[:, pl.ds(q_cols + kv_cols, kv_cols)], local_sem.at[2]
        ),
        pltpu.make_async_copy(hidden, hid.at[:, cols_of(t)], local_sem.at[3]),
    ]
    for load in loads:
        load.start()
    ids_all[...] = jnp.full_like(ids_all, -1)
    ids_row[...] = jnp.broadcast_to(ids_flat[...].reshape(1, tokens), (8, tokens))

    def upright(row):
        return jnp.transpose(jnp.broadcast_to(row, (128, 128)))

    for c in range(tokens // 128):
        here = slice(c * 128, (c + 1) * 128)
        piece = hidden[here, :].astype(jnp.float32)
        sums = jnp.sum(piece * piece, axis=1, keepdims=True)
        squares_own[:, here] = jnp.transpose(jnp.broadcast_to(sums, (128, 128)))[0:8, :]

    barrier = pltpu.get_barrier_semaphore()
    for d in range(1, back + 1):
        for other, there in ((place + d, place + d < n), (place - d, place >= d)):
            @pl.when(there)
            def _():
                pl.semaphore_signal(barrier, 1, device_id=(other, t), device_id_type=MESH)
    for k in range(1, 4):
        pl.semaphore_signal(barrier, 1, device_id=(place, (t + k) % 4), device_id_type=MESH)
    peers = 3
    for d in range(1, back + 1):
        peers = peers + jnp.where(place + d < n, 1, 0) + jnp.where(place >= d, 1, 0)
    pl.semaphore_wait(barrier, peers)

    def hid_copy(stream, c):
        rows = rows_of(c)
        if stream == 0:
            src, dst, to = hidden.at[rows], hid.at[rows, cols_of(t)], t1
        elif stream == 1:
            src, dst, to = hidden.at[rows], hid.at[rows, cols_of(t)], t2
        else:
            src, dst, to = hid.at[rows, cols_of(t2)], hid.at[rows, cols_of(t2)], t1
        return remote(src, dst, hid_send.at[stream, c], hid_recv.at[stream, c], (place, to))

    def hid_arrival(stream, c):
        rows = rows_of(c)
        dst = hid.at[rows, cols_of((t1, t2, t3)[stream])]
        return remote(dst, dst, hid_send.at[stream, c], hid_recv.at[stream, c], (place, t1))

    def ids_copy(d):
        return remote(
            ids_row, ids_all.at[d - 1], ids_send.at[d - 1], ids_recv.at[d - 1], (place + d, t)
        )

    for d in range(1, back + 1):
        @pl.when(place + d < n)
        def _():
            ids_copy(d).start()

    def squares_copy(k):
        return remote(
            squares_own, squares_in.at[t], sq_send.at[k], sq_recv.at[k], (place, (t + k) % 4)
        )

    for k in range(1, 4):
        squares_copy(k).start()

    def first_sends(c, carry):
        hid_copy(1, c).start()
        hid_copy(0, c).start()
        return carry

    lax.fori_loop(0, chunks, first_sends, 0)

    def block_at(h, c):
        return own.at[rows_of(c)] if h == 0 else line.at[h - 1, rows_of(c)]

    def line_copy(h, c):
        return remote(
            block_at(h, c), line.at[h, rows_of(c)],
            line_send.at[h, c], line_recv.at[h, c], (place + 2, t),
        )

    def line_goes(h):
        return (rank >= h) & (rank + 1 < ranks)

    def pair_copy(h, c):
        return remote(
            block_at(h, c), pair.at[h, rows_of(c)],
            pair_send.at[h, c], pair_recv.at[h, c], (mate, t),
        )

    def pair_goes(h, at):
        reach = 2 * h + 1 - 2 * at
        return (rank >= h) & (reach > 0) & (reach <= back)

    def direct(h, c):
        return (side == 1) | (c % 2 == 0) if h == 1 else True

    def relay_copy(c):
        return remote(
            pair.at[0, rows_of(c)], pair.at[1, rows_of(c)],
            relay_send.at[c], pair_recv.at[1, c], (place + 2, t),
        )

    def relays(c):
        return (side == 1) & (rank + 1 < ranks) & (c % 2 == 1)

    def pair_wait(h, c):
        block = pair.at[h, rows_of(c)]
        remote(block, block, pair_send.at[h, c], pair_recv.at[h, c], (place, t1)).wait_recv()

    def relay(c):
        @pl.when(relays(c))
        def _():
            pair_wait(0, c)
            relay_copy(c).start()

    def pass_on(h, c):
        if h < hops:
            @pl.when(line_goes(h))
            def _():
                line_copy(h, c).start()

        @pl.when(pair_goes(h, side) & direct(h, c))
        def _():
            pair_copy(h, c).start()

    def forward(h, c):
        @pl.when(rank >= h)
        def _():
            block = line.at[h - 1, rows_of(c)]
            remote(
                block, block, line_send.at[h - 1, c], line_recv.at[h - 1, c], (place, t1)
            ).wait_recv()
            pass_on(h, c)

    for d in range(1, back + 1):
        @pl.when(place >= d)
        def _():
            here = ids_all.at[d - 1]
            remote(here, here, ids_send.at[d - 1], ids_recv.at[d - 1], (place, t1)).wait_recv()

    gain[...] = jnp.broadcast_to(gain_flat[...].reshape(1, model), gain.shape)
    for c in range(tokens // 128):
        here = slice(c * 128, (c + 1) * 128)
        ids_col[here, :] = upright(ids_row[0:1, here].astype(jnp.float32)).astype(jnp.int32)
    first_id = ids_col[0:1, 0:1]
    prior = jnp.zeros((1, 1), jnp.float32)
    for d in range(back):
        same = jnp.where(ids_all[d, 0:1, :] == first_id, 1.0, 0.0)
        prior = prior + jnp.sum(same, axis=1, keepdims=True)

    def prepare(c, carry):
        rows = rows_of(c)
        ids_here = ids_col[rows, :]
        wide_ids = jnp.concatenate([ids_here] * (tokens // 128), axis=1)
        shape = (rows_in, tokens)
        earlier = lax.broadcasted_iota(jnp.int32, shape, 1) < (
            lax.broadcasted_iota(jnp.int32, shape, 0) + c * rows_in
        )
        local = jnp.where((wide_ids == ids_row[0:1, :]) & earlier, 1.0, 0.0)
        positions = jnp.sum(local, axis=1, keepdims=True) + jnp.where(
            ids_here == first_id, prior, 0.0
        )
        angles = positions * freqs[0:1, :]
        sine = jnp.sin(angles)
        cosines[rows, :] = jnp.cos(angles)
        sines[rows, :] = jnp.where(
            lax.broadcasted_iota(jnp.int32, sine.shape, 1) < HD // 2, -sine, sine
        )
        return carry

    lax.fori_loop(0, chunks, prepare, 0)
    numer[...] = jnp.zeros_like(numer)
    totals[...] = jnp.zeros_like(totals)
    own[...] = jnp.zeros_like(own)
    for k in range(1, 4):
        got = squares_in.at[(t + 4 - k) % 4]
        remote(got, got, sq_send.at[k], sq_recv.at[k], (place, t1)).wait_recv()
    squares = squares_own[0:1, :]
    for k in (t1, t2, t3):
        squares = squares + squares_in[k, 0:1, :]
    scale_row = lax.rsqrt(squares * (1.0 / model) + norm_eps)
    for c in range(tokens // 128):
        here = slice(c * 128, (c + 1) * 128)
        scales[here, :] = upright(scale_row[:, here])
    for load in loads:
        load.wait()
    near_cols = pl.ds(pl.multiple_of((t // 2) * half, 128), half)
    far_cols = pl.ds(pl.multiple_of((1 - t // 2) * half, 128), half)

    def normalized(rows, cols):
        piece = hid[rows, cols].astype(jnp.float32)
        return (piece * scales[rows, 0:1] * gain[0:1, cols]).astype(jnp.bfloat16)

    def near_norm(c, carry):
        hid_arrival(0, c).wait_recv()
        near[rows_of(c), :] = normalized(rows_of(c), near_cols)
        return carry

    lax.fori_loop(0, chunks, near_norm, 0)

    def near_dot(j, carry):
        cols = pl.ds(pl.multiple_of(j * 256, 256), 256)
        raw_near[:, cols] = jnp.dot(
            near[...], weights[near_cols, cols], preferred_element_type=jnp.float32
        )
        return carry

    lax.fori_loop(0, weights.shape[1] // 256, near_dot, 0)

    def attend_tile(block, id_row, group, at, size, causal):
        rows = pl.ds(pl.multiple_of(at * size, size), size)
        keys = block[:, pl.ds(pl.multiple_of(group * HD, HD), HD)]
        values = block[:, pl.ds(pl.multiple_of(kv_cols + group * HD, HD), HD)]
        allowed = jnp.concatenate([ids_col[rows, :]] * (tokens // 128), axis=1) == id_row
        if causal:
            shape = (size, tokens)
            allowed = allowed & (
                lax.broadcasted_iota(jnp.int32, shape, 1)
                <= lax.broadcasted_iota(jnp.int32, shape, 0) + at * size
            )
        for k in range(repeat):
            head = group * repeat + k
            scores = lax.dot_general(
                queries[head, rows, :], keys, (((1,), (1,)), ((), ())),
                preferred_element_type=jnp.float32,
            )
            raised = jnp.exp2(SCORE_OUT * jnp.tanh(scores * SCORE_IN))
            wts = jnp.where(allowed, raised, 0.0)
            part = wts[:, :128]
            for m in range(1, tokens // 128):
                part = part + wts[:, m * 128:(m + 1) * 128]
            totals[head, rows, :] += part
            numer[head, rows, :] += jnp.dot(
                wts.astype(jnp.bfloat16), values, preferred_element_type=jnp.float32
            )

    def project(c, carry):
        rows = rows_of(c)
        hid_arrival(1, c).wait_recv()
        hid_copy(2, c).start()
        hid_arrival(2, c).wait_recv()
        normed[...] = normalized(rows, far_cols)
        raw = raw_near[rows, :] + jnp.dot(
            normed[...], weights[far_cols, :], preferred_element_type=jnp.float32
        )
        cosine, sine = cosines[rows, :], sines[rows, :]

        def rotated(x):
            return (x * cosine + pltpu.roll(x, HD // 2, 1) * sine).astype(jnp.bfloat16)

        for j in range(kv_heads):
            at = q_cols + j * HD
            own[rows, j * HD:(j + 1) * HD] = rotated(raw[:, at:at + HD])
        own[rows, kv_cols:] = raw[:, q_cols + kv_cols:].astype(jnp.bfloat16)
        pass_on(0, c)
        for j in range(q_cols // HD):
            queries[j, rows, :] = rotated(raw[:, j * HD:(j + 1) * HD])
        for group in range(kv_heads):
            attend_tile(own, ids_row[0:1, :], group, c, rows_in, True)
        @pl.when(c >= 1)
        def _():
            relay(c - 1)
        for h in range(1, hops + 1):
            @pl.when(c >= h)
            def _():
                forward(h, c - h)
        return carry

    lax.fori_loop(0, chunks, project, 0)

    tile = min(256, tokens)

    def attend(block, id_row):
        def one(step, carry):
            group, at = step // (tokens // tile), step % (tokens // tile)
            attend_tile(block, id_row, group, at, tile, False)
            return carry

        lax.fori_loop(0, kv_heads * (tokens // tile), one, 0)

    def attend_line(h):
        if 2 * h > back:
            return

        @pl.when(rank >= h)
        def _():
            attend(line.at[h - 1], ids_all[2 * h - 1, 0:1, :])

    def attend_pair(h):
        @pl.when(pair_goes(h, 1 - side))
        def _():
            for c in range(chunks):
                if h == 0:
                    @pl.when(jnp.logical_not(relays(c)))
                    def _():
                        pair_wait(0, c)
                else:
                    pair_wait(h, c)
            attend(pair.at[h], ids_all[2 * h + 2 * side - 2, 0:1, :])

    relay(chunks - 1)
    for j in range(pages):
        picked = own[0:PAGE, :]
        for g in range(1, pages):
            picked = jnp.where(table[0, g] == j, own[g * PAGE:(g + 1) * PAGE, :], picked)
        staged[j] = picked

        @pl.when(t == j)
        def _():
            landed[j] = picked

    def cache_copy(k):
        j = (t + k) % 4
        return remote(
            staged.at[j], landed.at[t], cache_send.at[k], cache_recv.at[k], (place, j)
        )

    for k in range(1, 4):
        cache_copy(k).start()

    waiting = [("pair", 0)]
    for h in range(1, hops + 1):
        waiting += [("line", h), ("pair", h)]
    ready = 0
    for h in range(1, hops + 1):
        for later in range(h, hops + 1):
            forward(later, chunks - 1 + h - later)
        kind, index = waiting[ready]
        (attend_pair if kind == "pair" else attend_line)(index)
        ready += 1
    for kind, index in waiting[ready:]:
        (attend_pair if kind == "pair" else attend_line)(index)

    for head in range(q_cols // HD):
        total = jnp.sum(totals[head], axis=1, keepdims=True)
        attended[:, head * HD:(head + 1) * HD] = (numer[head] / total).astype(jnp.bfloat16)

    for k in range(1, 4):
        cache_copy(k).wait_send()
        squares_copy(k).wait_send()
        got = landed.at[(t + 4 - k) % 4]
        remote(got, got, cache_send.at[k], cache_recv.at[k], (place, t1)).wait_recv()
    for k in range(pages):
        for part in range(2):
            got = landed[k, :, part * kv_cols:(part + 1) * kv_cols].astype(jnp.float32)
            for m in range(kv_cols // 128):
                at = k * (kv_cols // 128) + m
                woven[at, pl.ds(part, PAGE, stride=2), :] = got[:, m * 128:(m + 1) * 128]
    for at in range(pages * kv_cols // 128):
        cache[:, at * 128:(at + 1) * 128] = woven[at].astype(jnp.bfloat16)

    def drain(c, carry):
        for stream in range(3):
            hid_copy(stream, c).wait_send()
        for h in range(hops + 1):
            if h < hops:
                @pl.when(line_goes(h))
                def _():
                    line_copy(h, c).wait_send()

            @pl.when(pair_goes(h, side) & direct(h, c))
            def _():
                pair_copy(h, c).wait_send()

        @pl.when(relays(c))
        def _():
            relay_copy(c).wait_send()
        return carry

    lax.fori_loop(0, chunks, drain, 0)
    for d in range(1, back + 1):
        @pl.when(place + d < n)
        def _():
            ids_copy(d).wait_send()


def per_device(n, hidden, norm_gain, w_query, w_key, w_value, segment_ids, page_table):
    tokens, width = hidden.shape
    model = norm_gain.shape[0]
    q_cols, kv_cols = w_query.shape[1], w_key.shape[1]
    pages = tokens // PAGE
    chunks = CHUNKS
    back = min(WIN // tokens, n - 1)
    hops = min(n // 2 - 1, (back + 1) // 2)
    half = HD // 2
    freqs = np.power(np.float32(10000.0), -(np.arange(half, dtype=np.float32) * np.float32(2.0 / HD)))
    freqs = np.tile(np.concatenate([freqs, freqs])[None, :], (8, 1)).astype(np.float32)
    vmem = pl.BlockSpec(memory_space=pltpu.VMEM)
    hbm = pl.BlockSpec(memory_space=pl.ANY)
    heads = q_cols // HD
    dma = pltpu.SemaphoreType.DMA
    attended, cache = pl.pallas_call(
        functools.partial(layer_kernel, n, back, hops, pages, chunks),
        out_shape=(
            jax.ShapeDtypeStruct((tokens, q_cols), jnp.bfloat16),
            jax.ShapeDtypeStruct((2 * PAGE, pages * kv_cols), jnp.bfloat16),
        ),
        in_specs=[
            vmem, vmem, hbm, hbm, hbm, vmem, vmem,
            pl.BlockSpec(memory_space=pltpu.SMEM),
        ],
        out_specs=(vmem, vmem),
        scratch_shapes=[
            pltpu.VMEM((8, model), jnp.float32),
            pltpu.VMEM((8, tokens), jnp.int32),
            pltpu.VMEM((tokens, 128), jnp.int32),
            pltpu.VMEM((tokens, HD), jnp.float32),
            pltpu.VMEM((tokens, HD), jnp.float32),
            pltpu.VMEM((pages * kv_cols // 128, 2 * PAGE, 128), jnp.float32),
            pltpu.VMEM((8, tokens), jnp.float32),
            pltpu.VMEM((4, 8, tokens), jnp.float32),
            pltpu.VMEM((tokens, 128), jnp.float32),
            pltpu.VMEM((tokens, q_cols + 2 * kv_cols), jnp.float32),
            pltpu.VMEM((tokens, 2 * width), jnp.bfloat16),
            pltpu.VMEM((tokens, model), jnp.bfloat16),
            pltpu.VMEM((model, q_cols + 2 * kv_cols), jnp.bfloat16),
            pltpu.VMEM((tokens // chunks, 2 * width), jnp.bfloat16),
            pltpu.VMEM((heads, tokens, HD), jnp.bfloat16),
            pltpu.VMEM((tokens, 2 * kv_cols), jnp.bfloat16),
            pltpu.VMEM((hops, tokens, 2 * kv_cols), jnp.bfloat16),
            pltpu.VMEM((hops + 1, tokens, 2 * kv_cols), jnp.bfloat16),
            pltpu.VMEM((back, 8, tokens), jnp.int32),
            pltpu.VMEM((heads, tokens, HD), jnp.float32),
            pltpu.VMEM((heads, tokens, 128), jnp.float32),
            pltpu.VMEM((pages, PAGE, 2 * kv_cols), jnp.bfloat16),
            pltpu.VMEM((pages, PAGE, 2 * kv_cols), jnp.bfloat16),
            dma((4,)),
            dma((3, chunks)), dma((3, chunks)),
            dma((hops, chunks)), dma((hops, chunks)),
            dma((hops + 1, chunks)), dma((hops + 1, chunks)),
            dma((back,)), dma((back,)),
            dma((4,)), dma((4,)),
            dma((4,)), dma((4,)), dma((chunks,)),
        ],
        compiler_params=pltpu.CompilerParams(
            collective_id=0, has_side_effects=True, vmem_limit_bytes=56 * 1024 * 1024
        ),
        cost_estimate=pl.CostEstimate(
            flops=2 * tokens * model * (q_cols + 2 * kv_cols)
            + 4 * heads * tokens * HD * tokens * (back + 1),
            bytes_accessed=2 * model * (q_cols + 2 * kv_cols),
            transcendentals=2 * heads * tokens * tokens * (back + 1),
        ),
    )(
        hidden, norm_gain, w_query, w_key, w_value, segment_ids, freqs, page_table
    )
    kv_cache = cache.reshape(1, PAGE, 2, pages * kv_cols)
    return (attended, kv_cache)


def solution(mesh):
    placed = (
        P("seq", "tp"),
        P(),
        P(None, "tp"),
        P(None, "tp"),
        P(None, "tp"),
        P("seq"),
        P("seq", None),
    )
    return jax.shard_map(
        functools.partial(per_device, mesh.shape["seq"]),
        mesh=mesh,
        in_specs=placed,
        out_specs=(P("seq", "tp"), P(("seq", "tp"), None, None, None)),
        check_vma=False,
    )
```
